32 devices in a mesh: seq: 4 (over z), dp: 2 (over y), mp: 4 (over x, core).
Axes of the slice: x: 2, y: 2, z: 4, core: 2. Of those that a mesh axis runs over, the one named last changes fastest.
Arguments:
- features: bfloat16 [2, 1024, 8, 512], P('dp', 'seq', None, 'mp'), may hold values from -6 to 6
- key_projection: bfloat16 [2, 1024, 8, 128], P('dp', 'seq'), may hold values from -2 to 2
- query_proj: bfloat16 [2, 1024, 8, 128], P('dp', 'seq'), may hold values from -2 to 2
- step_raw: float32 [2, 1024, 8, 8], P('dp', 'seq', None, 'mp'), may hold values from -3 to 6
- doc_starts: int32 [2, 1024], P('dp', 'seq'), may hold values 0 or 1
- log_rate: float32 [8, 8], P(None, 'mp'), may hold values from -5 to 1
- step_bias: float32 [8, 8], P(None, 'mp'), may hold values from -5 to -2.5
- skip_gain: float32 [8, 8], P(None, 'mp'), may hold values from 0.5 to 1.5
- out_grad: bfloat16 [2, 1024, 8, 512], P('dp', 'seq', None, 'mp'), may hold values from -6 to 6
Outputs:
- mixed_out: bfloat16 [2, 1024, 8, 512], P('dp', 'seq', None, 'mp')
- features_grad: bfloat16 [2, 1024, 8, 512], P('dp', 'seq', None, 'mp')
- key_grad: bfloat16 [2, 1024, 8, 128], P('dp', 'seq', 'mp')
- query_grad: bfloat16 [2, 1024, 8, 128], P('dp', 'seq', 'mp')
- step_grad: float32 [2, 1024, 8, 8], P('dp', 'seq', None, 'mp')
- log_rate_grad: float32 [8, 8], P(None, 'mp')
- step_bias_grad: float32 [8, 8], P(None, 'mp')
- skip_grad: float32 [8, 8], P(None, 'mp')
The draws below stay inside these ranges and needn't reach their ends.
All inputs are finite; a program needn't handle non-finite values. No bound on the sum of `doc_starts` on one device may be relied on, other than what follows from the above.
Results may differ from the reference program's by a relative error of at most 0.0015.
Values sent between devices are 32-bit elements; how exact they have to be, the bound alone decides.
A program may use at most 128 MiB of HBM per device.

```python
import math
import jax
import jax.numpy as jnp
from jax import lax

G = 8
HG = 8
P_SIZE = 64
N = 128
TOK_DEV = 256
BATCH_LINES = 2
SPAN_TOKENS = 1024


def draw_step_raw(key, part):
    starting_seed, jump_seed_handle = jax.random.split(key)
    full_shape = (BATCH_LINES, SPAN_TOKENS, G, HG)
    starting_entries = jnp.clip(0.7 * jax.random.normal(starting_seed, full_shape, jnp.float32), -3.0, 3.0)
    sudden_jumps = jax.random.bernoulli(jump_seed_handle, 3.0 / SPAN_TOKENS, (BATCH_LINES, SPAN_TOKENS, 1, 1))
    return starting_entries + jnp.where(sudden_jumps, 3.0, 0.0)


def set_ends(entries, own_key, smallest, top_value):
    longest = entries.shape.index(max(entries.shape))
    spots = []
    for shift in (0, 1):
        where = [jax.random.randint(jax.random.fold_in(own_key, axis), (), 0, length) for axis, length in enumerate(entries.shape)]
        where[longest] = (where[longest] + shift) % entries.shape[longest]
        spots.append(tuple(where))
    return entries.at[spots[0]].set(smallest).at[spots[1]].set(top_value)


def level_of(stream_key, dims, shards, smallest, high):
    def one(dim, shards_of):
        steps = jax.random.uniform(jax.random.fold_in(jax.random.fold_in(stream_key, 6), dim), (shards_of,), jnp.float32, smallest / len(shards), high / len(shards))
        return jnp.repeat(jnp.exp(steps), dims[dim] // shards_of).reshape((-1,) + (1,) * (len(dims) - dim - 1))

    level = one(*shards[0])
    for cut in shards[1:]:
        level = level * one(*cut)
    return level


def bell_draw(own_key, dims, spread, reach, cuts=(), dtype=jnp.bfloat16):
    entries = jax.random.normal(own_key, dims, jnp.float32) * spread
    if len(cuts) > 0:
        entries = level_of(own_key, dims, cuts, -0.22, 0.18) * entries
    return jnp.clip(entries, min=-reach, max=reach).astype(dtype)


def setup_inputs(seed: int = 0) -> dict:
    streams_of = jax.random.split(jax.random.key(seed), 10)
    features = bell_draw(streams_of[0], (BATCH_LINES, SPAN_TOKENS, G, HG * P_SIZE), 1.0, 6.0, ((0, 2), (1, 4), (3, 4)))
    key_projection = bell_draw(streams_of[1], (BATCH_LINES, SPAN_TOKENS, G, N), 0.3, 2.0, ((0, 2), (1, 4)))
    query_proj = bell_draw(streams_of[2], (BATCH_LINES, SPAN_TOKENS, G, N), 0.3, 2.0, ((0, 2), (1, 4)))
    step_raw = draw_step_raw(jax.random.fold_in(streams_of[9], 71), 0)
    doc_starts = set_ends((jax.random.randint(streams_of[4], (BATCH_LINES, SPAN_TOKENS), 0, 3 * TOK_DEV) < 1).astype(jnp.int32), jax.random.fold_in(streams_of[4], 1), 0, 1)
    log_rate = jnp.clip(-5.0 + 6.0 * jax.random.uniform(streams_of[5], (G, HG), jnp.float32) ** level_of(streams_of[5], (G, HG), ((1, 4),), -0.2, 0.2), -5.0, 1.0)
    step_bias = jnp.clip(-5.0 + 2.5 * jax.random.uniform(streams_of[6], (G, HG), jnp.float32) ** level_of(streams_of[6], (G, HG), ((1, 4),), -0.2, 0.2), -5.0, -2.5)
    skip_gain = jnp.clip(0.5 + 1.0 * jax.random.uniform(streams_of[7], (G, HG), jnp.float32) ** level_of(streams_of[7], (G, HG), ((1, 4),), -0.2, 0.2), 0.5, 1.5)
    out_grad = bell_draw(streams_of[8], (BATCH_LINES, SPAN_TOKENS, G, HG * P_SIZE), 1.0, 6.0, ((0, 2), (1, 4), (3, 4)))
    return dict(features=features, key_projection=key_projection, query_proj=query_proj, step_raw=step_raw, doc_starts=doc_starts, log_rate=log_rate, step_bias=step_bias, skip_gain=skip_gain, out_grad=out_grad)


precise = lax.Precision.HIGHEST

def decay_terms(step_raw, doc_starts, log_rate, step_bias):
    step_size = jax.nn.softplus(step_raw + step_bias)
    log_decay = -step_size * jnp.exp(log_rate)
    cumulative = jnp.cumsum(log_decay, axis=1)
    doc_count = jnp.cumsum(doc_starts, axis=1)
    return (step_size, cumulative, doc_count)

def block_forward(head_vals, key_vals, query_vals, step_raw, doc_starts, log_rate, step_bias, skip_gain, state_in):
    step_size, cumulative, doc_count = decay_terms(step_raw, doc_starts, log_rate, step_bias)
    block_len = head_vals.shape[1]
    causal = jnp.arange(block_len)[:, None] >= jnp.arange(block_len)[None, :]
    same_doc = causal[None] & (doc_count[:, :, None] == doc_count[:, None, :])
    doc_mask = same_doc[..., None, None]
    gap_log = cumulative[:, :, None] - cumulative[:, None, :]
    decay_mat = jnp.where(doc_mask, jnp.exp(jnp.where(doc_mask, gap_log, 0.0)), 0.0)
    entry_decay = jnp.where((doc_count == 0)[:, :, None, None], jnp.exp(cumulative), 0.0)
    scores = jnp.einsum('rtgn,rsgn->rtsg', query_vals, key_vals, precision=precise)
    mixing = scores[..., None] * decay_mat * step_size[:, None]
    output = jnp.einsum('rtsgh,rsghp->rtghp', mixing, head_vals, precision=precise)
    output = output + jnp.einsum('rtgn,rghpn->rtghp', query_vals, state_in, precision=precise) * entry_decay[..., None]
    output = output + skip_gain[..., None] * head_vals
    last_decay = decay_mat[:, -1]
    state_out = state_in * entry_decay[:, -1][..., None, None]
    state_out = state_out + jnp.einsum('rsgh,rsghp,rsgn->rghpn', last_decay * step_size, head_vals, key_vals, precision=precise)
    return (output, state_out)

def reference(features, key_projection, query_proj, step_raw, doc_starts, log_rate, step_bias, skip_gain, out_grad):
    row_count, length, groups, feat_width = features.shape
    head_count = feat_width // P_SIZE
    block_len = math.gcd(length, 128)
    block_count = length // block_len
    head_vals = features.astype(jnp.float32).reshape(row_count, length, groups, head_count, P_SIZE)
    key_vals = key_projection.astype(jnp.float32)
    query_vals = query_proj.astype(jnp.float32)

    def to_blocks(array):
        return jnp.moveaxis(array.reshape((row_count, block_count, block_len) + array.shape[2:]), 1, 0)

    def forward(head_vals, key_vals, query_vals, step_raw, log_rate, step_bias, skip_gain):

        def stepper(state, pieces):
            vals_b, keys_b, queries_b, raw_b, starts_b = pieces
            output, new_state = block_forward(vals_b, keys_b, queries_b, raw_b, starts_b, log_rate, step_bias, skip_gain, state)
            return (new_state, output)
        zero_state = jnp.zeros((row_count, groups, head_count, P_SIZE, N), jnp.float32)
        _, block_outs = lax.scan(jax.checkpoint(stepper), zero_state, (to_blocks(head_vals), to_blocks(key_vals), to_blocks(query_vals), to_blocks(step_raw), to_blocks(doc_starts)))
        return jnp.moveaxis(block_outs, 0, 1).reshape(row_count, length, groups, head_count, P_SIZE)
    mixed_vals, pullback = jax.vjp(forward, head_vals, key_vals, query_vals, step_raw, log_rate, step_bias, skip_gain)
    cotangent = out_grad.astype(jnp.float32).reshape(head_vals.shape)
    vals_grad, keys_grad, queries_grad, raw_grad, rate_grad, bias_grad, gain_grad = pullback(cotangent)
    return (mixed_vals.reshape(features.shape).astype(jnp.bfloat16), vals_grad.reshape(features.shape).astype(jnp.bfloat16), keys_grad.astype(jnp.bfloat16), queries_grad.astype(jnp.bfloat16), raw_grad, rate_grad, bias_grad, gain_grad)
```

```python
import functools

import jax
import jax.numpy as jnp
from jax import lax
from jax.experimental import pallas as pl
from jax.experimental.pallas import tpu as pltpu
from jax.sharding import PartitionSpec as P

P_SIZE = 64
F32 = jnp.float32
BF16 = jnp.bfloat16
MESH = pl.DeviceIdType.MESH
NN = ((1,), (0,))
NT = ((1,), (1,))


def mm(a, b, dims=NN):
    return lax.dot_general(a, b, (dims, ((), ())), preferred_element_type=F32)


def split2(a):
    hi = a.astype(BF16)
    return hi, (a - hi.astype(F32)).astype(BF16)


def split3(a):
    hi = a.astype(BF16)
    rest = a - hi.astype(F32)
    mid = rest.astype(BF16)
    return hi, mid, (rest - mid.astype(F32)).astype(BF16)


def left2(a, b, dims=NN):
    hi, lo = split2(a)
    return mm(hi, b, dims) + mm(lo, b, dims)


def right2(a, b, dims=NN):
    hi, lo = split2(b)
    return mm(a, hi, dims) + mm(a, lo, dims)


def left3(a, b, dims=NN):
    hi, mid, lo = split3(a)
    return mm(hi, b, dims) + mm(mid, b, dims) + mm(lo, b, dims)


def right3(a, b, dims=NN):
    hi, mid, lo = split3(b)
    return mm(a, hi, dims) + mm(a, mid, dims) + mm(a, lo, dims)


def both2(a, b, dims=NN):
    ah, al = split2(a)
    bh, bl = split2(b)
    return mm(ah, bh, dims) + mm(al, bh, dims) + mm(ah, bl, dims)


def kernel(
    nseq, ndp, nmp, L, G, H, N,
    x_ref, b_ref, c_ref, dy_ref, raw_ref, doc_ref, par_ref, skip_ref,
    y_out, dx_out, db_out, dc_out, step_out, small_out,
    wide, xg, bg, cg, gg, bt, ct, gt, tab, mask, prow,
    loc_f, loc_b, s_in, s_out, d_out, d_in,
    ybuf, dxbuf, part, rows_r, rows_k, zrow, skiprow,
    rbuf, sbuf,
    f_send, f_recv, b_send, b_recv, m_send, m_recv, p_send, p_recv,
):
    hp = H * P_SIZE
    gl = G // nmp
    npar = nseq * ndp
    gh = G * H
    me_s, me_d, me_m = lax.axis_index("seq"), lax.axis_index("dp"), lax.axis_index("mp")
    me_p = me_s * ndp + me_d
    last = nseq - 1

    barrier = pltpu.get_barrier_semaphore()

    @pl.loop(1, nmp)
    def _(j):
        pl.semaphore_signal(
            barrier, inc=1, device_id={"mp": lax.rem(me_m + j, nmp)}, device_id_type=MESH
        )

    @pl.loop(1, npar)
    def _(j):
        to = lax.rem(me_p + j, npar)
        pl.semaphore_signal(
            barrier,
            inc=1,
            device_id={"seq": to // ndp, "dp": lax.rem(to, ndp)},
            device_id_type=MESH,
        )

    for src, dst in ((x_ref, xg), (b_ref, bg), (c_ref, cg), (dy_ref, gg)):
        width = src.shape[1]
        wide[:, :width] = src[...].astype(F32)
        for g in range(G):
            block = wide[pl.ds(g, L, stride=G), :width]
            dst[g] = block.astype(BF16)
            if dst is bg:
                bt[g] = block.T.astype(BF16)
            if dst is cg:
                ct[g] = block.T.astype(BF16)
            if dst is gg:
                gt[g] = block.T.astype(BF16)

    i0 = lax.broadcasted_iota(jnp.int32, (L, L), 0)
    i1 = lax.broadcasted_iota(jnp.int32, (L, L), 1)
    upper = jnp.where(i0 <= i1, 1.0, 0.0).astype(BF16)
    raw = raw_ref[...]
    log_rate, bias = par_ref[:, 0:1], par_ref[:, 1:2]
    z = raw + bias
    dt = jnp.maximum(z, 0.0) + jnp.log1p(jnp.exp(-jnp.abs(z)))
    rate = jnp.exp(log_rate)
    cum = left3(-dt * rate, upper)
    docs = mm(jnp.broadcast_to(doc_ref[...].astype(F32), (8, L)).astype(BF16), upper)
    doc_row = docs[0:1]
    entry = jnp.where(doc_row == 0.0, jnp.exp(cum), 0.0)
    tail = doc_row == doc_row[:, L - 1 : L]
    weight = jnp.where(tail, jnp.exp(cum[:, L - 1 : L] - cum), 0.0) * dt
    doc_col = docs.T[:, 0:1]
    mask[...] = jnp.where((i0 >= i1) & (doc_col == doc_row), 0.0, -1e30)
    lane_head = lax.broadcasted_iota(jnp.int32, (1, hp), 1) // P_SIZE
    for g in range(G):
        for q, val in enumerate((cum, dt, weight, entry)):
            tab[g, q * H : (q + 1) * H, :] = val[g * H : (g + 1) * H]
        passed = entry[g * H : g * H + 1, L - 1 : L]
        passed = jnp.broadcast_to(passed, (1, hp))
        for h in range(1, H):
            passed = jnp.where(
                lane_head == h, entry[g * H + h : g * H + h + 1, L - 1 : L], passed
            )
        prow[g] = passed

    lanes_l = lax.broadcasted_iota(jnp.int32, (L, hp), 1) // P_SIZE

    def spread(cols, first):
        val = jnp.broadcast_to(cols[:, first : first + 1], (L, hp))
        for h in range(1, H):
            val = jnp.where(lanes_l == h, cols[:, first + h : first + h + 1], val)
        return val

    def send_f(g):
        return pltpu.make_async_remote_copy(
            src_ref=s_out.at[g], dst_ref=s_in.at[g],
            send_sem=f_send.at[g], recv_sem=f_recv.at[g],
            device_id={"seq": jnp.minimum(me_s + 1, last)}, device_id_type=MESH,
        )

    def send_b(g):
        return pltpu.make_async_remote_copy(
            src_ref=d_in.at[g], dst_ref=d_out.at[g],
            send_sem=b_send.at[g], recv_sem=b_recv.at[g],
            device_id={"seq": jnp.maximum(me_s - 1, 0)}, device_id_type=MESH,
        )

    def send_m(g, j):
        return pltpu.make_async_remote_copy(
            src_ref=part.at[g], dst_ref=rbuf.at[lax.rem(g, gl), j],
            send_sem=m_send.at[g], recv_sem=m_recv.at[lax.rem(g, gl), j],
            device_id={"mp": g // gl}, device_id_type=MESH,
        )

    pl.semaphore_wait(barrier, (nmp - 1) + (npar - 1))

    @pl.loop(0, G)
    def _(g):
        cols = tab[g].T
        loc_f[g] = right2(bt[g], xg[g].astype(F32) * spread(cols, 2 * H))
        loc_b[g] = right2(ct[g], gg[g].astype(F32) * spread(cols, 3 * H))

        @pl.when(me_s == 0)
        def _():
            s_in[g] = jnp.zeros((N, hp), F32)
            s_out[g] = loc_f[g]
            if nseq > 1:
                send_f(g).start()

        @pl.when(me_s == last)
        def _():
            d_out[g] = jnp.zeros((N, hp), F32)
            d_in[g] = loc_b[g]
            if nseq > 1:
                send_b(g).start()

    def local(g):
        cols = tab[g].T
        trow = tab[g]
        xb, bb, cb, gb = xg[g], bg[g], cg[g], gg[g]
        scores = mm(cb, bt[g])
        grad_s = None
        y = None
        dxt = []
        pr = jnp.zeros((8, L), F32)
        head_row = lax.broadcasted_iota(jnp.int32, (8, 128), 0)
        for h in range(H):
            xm = jnp.where(lanes_l == h, xb.astype(F32), 0.0).astype(BF16)
            dm = mm(gb, xm, NT)
            decay = jnp.exp(cols[:, h : h + 1] - trow[h : h + 1] + mask[...])
            w = decay * trow[H + h : H + h + 1]
            mix = scores * w
            dmw = dm * w
            grad_s = dmw if grad_s is None else grad_s + dmw
            q = dmw * scores
            rows_k[g, h : h + 1, :] = jnp.sum(q, axis=0, keepdims=True)
            folded = q[:, 0:128]
            for j in range(128, L, 128):
                folded = folded + q[:, j : j + 128]
            pick = jnp.where(head_row == h, 1.0, 0.0).astype(BF16)
            pr = pr + right3(pick, folded, NT)
            hi, lo = split2(mix)
            now = mm(hi, xm) + mm(lo, xm)
            y = now if y is None else y + now
            gth = gt[g, h * P_SIZE : (h + 1) * P_SIZE, :]
            dxt.append(mm(gth, hi) + mm(gth, lo))
        rows_r[g] = pr
        ybuf[g] = y
        dxbuf[g] = (dxt[0] if H == 1 else jnp.concatenate(dxt, axis=0)).T
        hi, lo = split2(grad_s)
        part[g, 1] = mm(hi, bb) + mm(lo, bb)
        part[g, 0] = (mm(ct[g], hi) + mm(ct[g], lo)).T

    head8 = lax.broadcasted_iota(jnp.int32, (8, hp), 0)
    sel = jnp.where(head8 == lax.broadcasted_iota(jnp.int32, (8, hp), 1) // P_SIZE, 1.0, 0.0)
    sel = sel.astype(BF16)

    def finish(g):
        cols = tab[g].T
        wl, el = spread(cols, 2 * H), spread(cols, 3 * H)
        xb, bb, cb, gb = xg[g], bg[g], cg[g], gg[g]
        xf, gf = xb.astype(F32), gb.astype(F32)
        sin, dso = s_in[g], d_out[g]
        gain = skip_ref[pl.ds(g, 1), :]
        yo = right2(cb, sin) * el
        dxo = right2(bb, dso) * wl
        ybuf[g] = ybuf[g] + yo + gain * xf
        dxbuf[g] = dxbuf[g] + dxo + gain * gf
        e_rows = right3(sel, gf * yo, NT)
        f_rows = right3(sel, xf * dxo, NT)
        rows_r[g] = rows_r[g] + e_rows
        rows_k[g, 0:H, :] = rows_k[g, 0:H, :] + f_rows[0:H]
        part[g, 1] = part[g, 1] + both2(gf * el, sin, NT)
        part[g, 0] = part[g, 0] + both2(xf * wl, dso, NT)
        skiprow[g] = jnp.sum(gf * xf, axis=0, keepdims=True)
        zrow[g] = jnp.sum((prow[g] * sin + loc_f[g]) * dso, axis=0, keepdims=True)

        @pl.when(g // gl != me_m)
        def _():
            send_m(g, me_m).start()

    lag_f = me_s - 1
    lag_b = last - me_s - 1
    lag = jnp.maximum(jnp.maximum(lag_f, lag_b), 0)

    @pl.loop(0, G + max(nseq - 2, 0))
    def _(i):
        @pl.when(i < G)
        def _():
            local(i)

        if nseq > 1:
            gf = i - lag_f
            gb = i - lag_b

            @pl.when((me_s > 0) & (gf >= 0) & (gf < G))
            def _():
                send_f(gf).wait_recv()

                @pl.when(me_s < last)
                def _():
                    s_out[gf] = prow[gf] * s_in[gf] + loc_f[gf]
                    send_f(gf).start()

            @pl.when((me_s < last) & (gb >= 0) & (gb < G))
            def _():
                send_b(gb).wait_recv()

                @pl.when(me_s > 0)
                def _():
                    d_in[gb] = prow[gb] * d_out[gb] + loc_b[gb]
                    send_b(gb).start()

        g = i - lag

        @pl.when((g >= 0) & (g < G))
        def _():
            finish(g)

    k_all = jnp.concatenate([rows_k[g, 0:H, :] for g in range(G)], axis=0)
    r_all = jnp.concatenate([rows_r[g, 0:H, :] for g in range(G)], axis=0)
    zcol = jnp.concatenate(
        [
            jnp.sum(jnp.where(lane_head == h, zrow[g], 0.0), axis=1, keepdims=True)
            for g in range(G)
            for h in range(H)
        ],
        axis=0,
    )
    dld = left3(r_all - k_all, upper, NT) + zcol
    ddt = k_all / dt - rate * dld
    dz = ddt * (1.0 / (1.0 + jnp.exp(-z)))
    step_out[...] = dz
    rate_g = -jnp.sum(dld * dt, axis=1, keepdims=True) * rate
    bias_g = jnp.sum(dz, axis=1, keepdims=True)
    lane = lax.broadcasted_iota(jnp.int32, (gh, 128), 1)
    mine = jnp.where(lane == 0, rate_g, jnp.where(lane == 1, bias_g, 0.0))
    skip_all = jnp.concatenate([skiprow[g] for g in range(G)], axis=0)
    if hp < 128:
        skip_all = jnp.concatenate([skip_all, jnp.zeros((G, 128 - hp), F32)], axis=1)
    sbuf[me_p] = jnp.concatenate([mine, skip_all], axis=0)

    def send_p(j):
        to = lax.rem(me_p + j, npar)
        return pltpu.make_async_remote_copy(
            src_ref=sbuf.at[me_p], dst_ref=sbuf.at[me_p],
            send_sem=p_send.at[j], recv_sem=p_recv.at[me_p],
            device_id={"seq": to // ndp, "dp": lax.rem(to, ndp)}, device_id_type=MESH,
        )

    @pl.loop(1, npar)
    def _(j):
        send_p(j).start()

    for buf, dst in ((ybuf, y_out), (dxbuf, dx_out)):
        for g in range(G):
            wide[pl.ds(g, L, stride=G), :hp] = buf[g]
        dst[...] = wide[:, :hp].astype(BF16)

    for a in range(gl):
        g = me_m * gl + a

        @pl.loop(1, nmp)
        def _(j):
            frm = lax.rem(me_m + j, nmp)
            pltpu.make_async_copy(part.at[g], rbuf.at[a, frm], m_recv.at[a, frm]).wait()
            part[g] = part[g] + rbuf[a, frm]

        db_out[:, a * N : (a + 1) * N] = part[g, 0].astype(BF16)
        dc_out[:, a * N : (a + 1) * N] = part[g, 1].astype(BF16)

    @pl.loop(1, npar)
    def _(j):
        frm = lax.rem(me_p + j, npar)
        pltpu.make_async_copy(sbuf.at[frm], sbuf.at[frm], p_recv.at[frm]).wait()

    total = sbuf[0]
    for j in range(1, npar):
        total = total + sbuf[j]
    small_out[...] = total

    @pl.loop(1, npar)
    def _(j):
        send_p(j).wait_send()

    @pl.loop(0, G)
    def _(g):
        @pl.when(g // gl != me_m)
        def _():
            send_m(g, me_m).wait_send()

        if nseq > 1:

            @pl.when(me_s < last)
            def _():
                send_f(g).wait_send()

            @pl.when(me_s > 0)
            def _():
                send_b(g).wait_send()


def local(
    nseq, ndp, nmp,
    features, key_projection, query_proj, step_raw, doc_starts,
    log_rate, step_bias, skip_gain, out_grad,
):
    rows, L, G, hp = features.shape
    assert rows == 1
    N = key_projection.shape[-1]
    H = hp // P_SIZE
    gl = G // nmp
    gh = G * H
    npar = nseq * ndp
    raw = jnp.transpose(step_raw[0], (1, 2, 0)).reshape(gh, L)
    par = jnp.stack([log_rate.reshape(gh), step_bias.reshape(gh)], axis=-1)
    gain = jnp.repeat(skip_gain, P_SIZE, axis=1)
    vm = pltpu.VMEM
    nr = -(-4 * H // 8) * 8
    dma = pltpu.SemaphoreType.DMA
    scratch = [
        vm((L * G, max(hp, N)), F32),
        vm((G, L, hp), BF16), vm((G, L, N), BF16), vm((G, L, N), BF16), vm((G, L, hp), BF16),
        vm((G, N, L), BF16), vm((G, N, L), BF16), vm((G, hp, L), BF16),
        vm((G, nr, L), F32), vm((L, L), F32), vm((G, 1, hp), F32),
        vm((G, N, hp), F32), vm((G, N, hp), F32),
        vm((G, N, hp), F32), vm((G, N, hp), F32), vm((G, N, hp), F32), vm((G, N, hp), F32),
        vm((G, L, hp), F32), vm((G, L, hp), F32), vm((G, 2, L, N), F32),
        vm((G, 8, L), F32), vm((G, 8, L), F32), vm((G, 1, hp), F32), vm((G, 1, hp), F32),
        vm((gl, nmp, 2, L, N), F32), vm((npar, gh + G, 128), F32),
        dma((G,)), dma((G,)), dma((G,)), dma((G,)), dma((G,)), dma((gl, nmp)),
        dma((npar,)), dma((npar,)),
    ]
    y, dx, db, dc, step, small = pl.pallas_call(
        functools.partial(kernel, nseq, ndp, nmp, L, G, H, N),
        out_shape=(
            jax.ShapeDtypeStruct((L * G, hp), BF16),
            jax.ShapeDtypeStruct((L * G, hp), BF16),
            jax.ShapeDtypeStruct((L, gl * N), BF16),
            jax.ShapeDtypeStruct((L, gl * N), BF16),
            jax.ShapeDtypeStruct((gh, L), F32),
            jax.ShapeDtypeStruct((gh + G, 128), F32),
        ),
        in_specs=[pl.BlockSpec(memory_space=pltpu.VMEM)] * 8,
        out_specs=[pl.BlockSpec(memory_space=pltpu.VMEM)] * 6,
        scratch_shapes=scratch,
        compiler_params=pltpu.CompilerParams(
            collective_id=0, has_side_effects=True, vmem_limit_bytes=56 * 2**20
        ),
    )(
        features.reshape(L * G, hp),
        key_projection.reshape(L * G, N),
        query_proj.reshape(L * G, N),
        out_grad.reshape(L * G, hp),
        raw, doc_starts, par, gain,
    )
    return (
        y.reshape(1, L, G, hp),
        dx.reshape(1, L, G, hp),
        db.reshape(1, L, gl, N),
        dc.reshape(1, L, gl, N),
        jnp.transpose(step.reshape(G, H, L), (2, 0, 1))[None],
        small[:gh, 0].reshape(G, H),
        small[:gh, 1].reshape(G, H),
        small[gh:, :hp].reshape(G, H, P_SIZE).sum(-1),
    )


def solution(mesh):
    sizes = dict(mesh.shape)
    return jax.shard_map(
        functools.partial(local, sizes["seq"], sizes["dp"], sizes["mp"]),
        mesh=mesh,
        in_specs=(
            P("dp", "seq", None, "mp"),
            P("dp", "seq", None, None),
            P("dp", "seq", None, None),
            P("dp", "seq", None, "mp"),
            P("dp", "seq"),
            P(None, "mp"),
            P(None, "mp"),
            P(None, "mp"),
            P("dp", "seq", None, "mp"),
        ),
        out_specs=(
            P("dp", "seq", None, "mp"),
            P("dp", "seq", None, "mp"),
            P("dp", "seq", "mp", None),
            P("dp", "seq", "mp", None),
            P("dp", "seq", None, "mp"),
            P(None, "mp"),
            P(None, "mp"),
            P(None, "mp"),
        ),
        check_vma=False,
    )
```

```python
import functools

import jax
import jax.numpy as jnp
from jax import lax
from jax.experimental import pallas as pl
from jax.experimental.pallas import tpu as pltpu
from jax.sharding import PartitionSpec as P

P_SIZE = 64
F32 = jnp.float32
BF16 = jnp.bfloat16
MESH = pl.DeviceIdType.MESH
NN = ((1,), (0,))
NT = ((1,), (1,))


def mm(a, b, dims=NN):
    return lax.dot_general(a, b, (dims, ((), ())), preferred_element_type=F32)


def split2(a):
    hi = a.astype(BF16)
    return hi, (a - hi.astype(F32)).astype(BF16)


def split3(a):
    hi = a.astype(BF16)
    rest = a - hi.astype(F32)
    mid = rest.astype(BF16)
    return hi, mid, (rest - mid.astype(F32)).astype(BF16)


def left2(a, b, dims=NN):
    hi, lo = split2(a)
    return mm(hi, b, dims) + mm(lo, b, dims)


def right2(a, b, dims=NN):
    hi, lo = split2(b)
    return mm(a, hi, dims) + mm(a, lo, dims)


def left3(a, b, dims=NN):
    hi, mid, lo = split3(a)
    return mm(hi, b, dims) + mm(mid, b, dims) + mm(lo, b, dims)


def right3(a, b, dims=NN):
    hi, mid, lo = split3(b)
    return mm(a, hi, dims) + mm(a, mid, dims) + mm(a, lo, dims)


def both2(a, b, dims=NN):
    ah, al = split2(a)
    bh, bl = split2(b)
    return mm(ah, bh, dims) + mm(al, bh, dims) + mm(ah, bl, dims)


def kernel(
    nseq, ndp, nmp, L, G, H, N,
    x_ref, b_ref, c_ref, dy_ref, raw_ref, doc_ref, rate_ref, bias_ref, skip_ref,
    y_out, dx_out, db_out, dc_out, step_out, small_out,
    pars, gains,
    wide, xg, bg, cg, gg, bt, ct, gt, tab, mask, prow,
    loc_f, loc_b, s_in, s_out, d_out, d_in,
    ybuf, dxbuf, part, rows_r, rows_k, zrow, skiprow,
    xbuf, rbuf, sbuf,
    f_send, f_recv, b_send, b_recv, x_send, x_recv, m_send, m_recv, p_send, p_recv,
):
    hp = H * P_SIZE
    gl = G // nmp
    npar = nseq * ndp
    gh = G * H
    me_s, me_d, me_m = lax.axis_index("seq"), lax.axis_index("dp"), lax.axis_index("mp")
    me_p = me_s * ndp + me_d
    last = nseq - 1
    fan = 2 if nmp % 2 == 0 else 1
    pairs = nmp // fan
    me_x, me_c = me_m // fan, lax.rem(me_m, fan)

    def at(p):
        return lax.rem(p + (me_x + 1) * (gl * fan), G)


    barrier = pltpu.get_barrier_semaphore()

    @pl.loop(1, nmp)
    def _(j):
        pl.semaphore_signal(
            barrier, inc=1, device_id={"mp": lax.rem(me_m + j, nmp)}, device_id_type=MESH
        )

    @pl.loop(1, npar)
    def _(j):
        to = lax.rem(me_p + j, npar)
        pl.semaphore_signal(
            barrier,
            inc=1,
            device_id={"seq": to // ndp, "dp": lax.rem(to, ndp)},
            device_id_type=MESH,
        )

    for src, dst in ((x_ref, xg), (b_ref, bg), (c_ref, cg), (dy_ref, gg)):
        width = src.shape[1]
        wide[:, :width] = src[...].astype(F32)
        for g in range(G):
            block = wide[pl.ds(g, L, stride=G), :width]
            dst[g] = block.astype(BF16)
            if dst is bg:
                bt[g] = block.T.astype(BF16)
            if dst is cg:
                ct[g] = block.T.astype(BF16)
            if dst is gg:
                gt[g] = block.T.astype(BF16)

    i0 = lax.broadcasted_iota(jnp.int32, (L, L), 0)
    i1 = lax.broadcasted_iota(jnp.int32, (L, L), 1)
    upper = jnp.where(i0 <= i1, 1.0, 0.0).astype(BF16)
    raw = jnp.concatenate([raw_ref[g, h : h + 1, :] for h in range(H) for g in range(G)], axis=0)
    pars[...] = jnp.zeros_like(pars)
    for q, ref in enumerate((rate_ref, bias_ref, skip_ref)):
        pars[q * H : (q + 1) * H, 0:G] = ref[...]
    turned = pars[...].T
    log_rate = jnp.concatenate([turned[0:G, h : h + 1] for h in range(H)], axis=0)
    bias = jnp.concatenate([turned[0:G, H + h : H + h + 1] for h in range(H)], axis=0)
    z = raw + bias
    dt = jnp.maximum(z, 0.0) + jnp.log1p(jnp.exp(-jnp.abs(z)))
    rate = jnp.exp(log_rate)
    cum = left3(-dt * rate, upper)
    docs = mm(jnp.broadcast_to(doc_ref[...].astype(F32), (8, L)).astype(BF16), upper)
    doc_row = docs[0:1]
    entry = jnp.where(doc_row == 0.0, jnp.exp(cum), 0.0)
    tail = doc_row == doc_row[:, L - 1 : L]
    weight = jnp.where(tail, jnp.exp(cum[:, L - 1 : L] - cum), 0.0) * dt
    doc_col = docs.T[:, 0:1]
    mask[...] = jnp.where((i0 >= i1) & (doc_col == doc_row), 0.0, -1e30)
    lane_head = lax.broadcasted_iota(jnp.int32, (1, hp), 1) // P_SIZE
    for g in range(G):
        for q, val in enumerate((cum, dt, weight, entry)):
            for h in range(H):
                tab[g, q * H + h : q * H + h + 1, :] = val[h * G + g : h * G + g + 1]
        passed = entry[g : g + 1, L - 1 : L]
        passed = jnp.broadcast_to(passed, (1, hp))
        for h in range(1, H):
            passed = jnp.where(
                lane_head == h, entry[h * G + g : h * G + g + 1, L - 1 : L], passed
            )
        prow[g] = passed
    gain = jnp.broadcast_to(turned[0:G, 2 * H : 2 * H + 1], (G, hp))
    for h in range(1, H):
        gain = jnp.where(lane_head == h, turned[0:G, 2 * H + h : 2 * H + h + 1], gain)
    gains[...] = gain

    lanes_l = lax.broadcasted_iota(jnp.int32, (L, hp), 1) // P_SIZE

    def spread(cols, first):
        val = jnp.broadcast_to(cols[:, first : first + 1], (L, hp))
        for h in range(1, H):
            val = jnp.where(lanes_l == h, cols[:, first + h : first + h + 1], val)
        return val

    def send_f(g):
        return pltpu.make_async_remote_copy(
            src_ref=s_out.at[g], dst_ref=s_in.at[g],
            send_sem=f_send.at[g], recv_sem=f_recv.at[g],
            device_id={"seq": jnp.minimum(me_s + 1, last)}, device_id_type=MESH,
        )

    def send_b(g):
        return pltpu.make_async_remote_copy(
            src_ref=d_in.at[g], dst_ref=d_out.at[g],
            send_sem=b_send.at[g], recv_sem=b_recv.at[g],
            device_id={"seq": jnp.maximum(me_s - 1, 0)}, device_id_type=MESH,
        )

    def send_x(g):
        return pltpu.make_async_remote_copy(
            src_ref=part.at[g], dst_ref=xbuf.at[g],
            send_sem=x_send.at[g], recv_sem=x_recv.at[g],
            device_id={"mp": me_x * fan + (fan - 1 - me_c)}, device_id_type=MESH,
        )

    def send_m(g):
        return pltpu.make_async_remote_copy(
            src_ref=part.at[g], dst_ref=rbuf.at[lax.rem(g, gl), me_x],
            send_sem=m_send.at[g], recv_sem=m_recv.at[lax.rem(g, gl), me_x],
            device_id={"mp": g // gl}, device_id_type=MESH,
        )

    def mine_c(g):
        return lax.rem(g // gl, fan) == me_c

    def mine_x(g):
        return g // (gl * fan) == me_x

    pl.semaphore_wait(barrier, (nmp - 1) + (npar - 1))

    @pl.loop(0, G)
    def _(p):
        g = at(p)
        cols = tab[g].T
        loc_f[g] = right2(bt[g], xg[g].astype(F32) * spread(cols, 2 * H))
        loc_b[g] = right2(ct[g], gg[g].astype(F32) * spread(cols, 3 * H))

        @pl.when(me_s == 0)
        def _():
            s_in[g] = jnp.zeros((N, hp), F32)
            s_out[g] = loc_f[g]
            if nseq > 1:
                send_f(g).start()

        @pl.when(me_s == last)
        def _():
            d_out[g] = jnp.zeros((N, hp), F32)
            d_in[g] = loc_b[g]
            if nseq > 1:
                send_b(g).start()

    def local(g):
        cols = tab[g].T
        trow = tab[g]
        xb, bb, cb, gb = xg[g], bg[g], cg[g], gg[g]
        scores = mm(cb, bt[g])
        grad_s = None
        y = None
        dxt = []
        pr = jnp.zeros((8, L), F32)
        head_row = lax.broadcasted_iota(jnp.int32, (8, 128), 0)
        for h in range(H):
            xm = jnp.where(lanes_l == h, xb.astype(F32), 0.0).astype(BF16)
            dm = mm(gb, xm, NT)
            decay = jnp.exp(cols[:, h : h + 1] - trow[h : h + 1] + mask[...])
            w = decay * trow[H + h : H + h + 1]
            mix = scores * w
            dmw = dm * w
            grad_s = dmw if grad_s is None else grad_s + dmw
            q = dmw * scores
            rows_k[g, h : h + 1, :] = jnp.sum(q, axis=0, keepdims=True)
            folded = q[:, 0:128]
            for j in range(128, L, 128):
                folded = folded + q[:, j : j + 128]
            pick = jnp.where(head_row == h, 1.0, 0.0).astype(BF16)
            pr = pr + right3(pick, folded, NT)
            hi, lo = split2(mix)
            now = mm(hi, xm) + mm(lo, xm)
            y = now if y is None else y + now
            gth = gt[g, h * P_SIZE : (h + 1) * P_SIZE, :]
            dxt.append(mm(gth, hi) + mm(gth, lo))
        rows_r[g] = pr
        ybuf[g] = y
        dxbuf[g] = (dxt[0] if H == 1 else jnp.concatenate(dxt, axis=0)).T
        hi, lo = split2(grad_s)
        part[g, 1] = mm(hi, bb) + mm(lo, bb)
        part[g, 0] = (mm(ct[g], hi) + mm(ct[g], lo)).T

    head8 = lax.broadcasted_iota(jnp.int32, (8, hp), 0)
    sel = jnp.where(head8 == lax.broadcasted_iota(jnp.int32, (8, hp), 1) // P_SIZE, 1.0, 0.0)
    sel = sel.astype(BF16)

    def finish(g):
        cols = tab[g].T
        wl, el = spread(cols, 2 * H), spread(cols, 3 * H)
        xb, bb, cb, gb = xg[g], bg[g], cg[g], gg[g]
        xf, gf = xb.astype(F32), gb.astype(F32)
        sin, dso = s_in[g], d_out[g]
        gain = gains[pl.ds(g, 1), :]
        yo = right2(cb, sin) * el
        dxo = right2(bb, dso) * wl
        ybuf[g] = ybuf[g] + yo + gain * xf
        dxbuf[g] = dxbuf[g] + dxo + gain * gf
        e_rows = right3(sel, gf * yo, NT)
        f_rows = right3(sel, xf * dxo, NT)
        rows_r[g] = rows_r[g] + e_rows
        rows_k[g, 0:H, :] = rows_k[g, 0:H, :] + f_rows[0:H]
        part[g, 1] = part[g, 1] + both2(gf * el, sin, NT)
        part[g, 0] = part[g, 0] + both2(xf * wl, dso, NT)
        skiprow[g] = jnp.sum(gf * xf, axis=0, keepdims=True)
        zrow[g] = jnp.sum((prow[g] * sin + loc_f[g]) * dso, axis=0, keepdims=True)

        if fan > 1:

            @pl.when(jnp.logical_not(mine_c(g)))
            def _():
                send_x(g).start()

    def across(g):
        @pl.when(mine_c(g))
        def _():
            if fan > 1:
                send_x(g).wait_recv()
                part[g] = part[g] + xbuf[g]
            if pairs > 1:

                @pl.when(jnp.logical_not(mine_x(g)))
                def _():
                    send_m(g).start()

    lag_f = me_s - 1
    lag_b = last - me_s - 1
    lag = jnp.maximum(jnp.maximum(lag_f, lag_b), 0)

    @pl.loop(0, G + max(nseq - 2, 0) + 1)
    def _(i):
        @pl.when(i < G)
        def _():
            local(at(i))

        if nseq > 1:
            pf = i - lag_f
            pb = i - lag_b

            @pl.when((me_s > 0) & (pf >= 0) & (pf < G))
            def _():
                gf = at(pf)
                send_f(gf).wait_recv()

                @pl.when(me_s < last)
                def _():
                    s_out[gf] = prow[gf] * s_in[gf] + loc_f[gf]
                    send_f(gf).start()

            @pl.when((me_s < last) & (pb >= 0) & (pb < G))
            def _():
                gb = at(pb)
                send_b(gb).wait_recv()

                @pl.when(me_s > 0)
                def _():
                    d_in[gb] = prow[gb] * d_out[gb] + loc_b[gb]
                    send_b(gb).start()

        p = i - lag

        @pl.when((p >= 0) & (p < G))
        def _():
            finish(at(p))

        @pl.when((p >= 1) & (p <= G))
        def _():
            across(at(p - 1))

    k_all = jnp.concatenate([rows_k[g, h : h + 1, :] for h in range(H) for g in range(G)], axis=0)
    r_all = jnp.concatenate([rows_r[g, h : h + 1, :] for h in range(H) for g in range(G)], axis=0)
    zcol = jnp.concatenate(
        [
            jnp.sum(jnp.where(lane_head == h, zrow[g], 0.0), axis=1, keepdims=True)
            for h in range(H)
            for g in range(G)
        ],
        axis=0,
    )
    dld = left3(r_all - k_all, upper, NT) + zcol
    ddt = k_all / dt - rate * dld
    dz = ddt * (1.0 / (1.0 + jnp.exp(-z)))
    for g in range(G):
        for h in range(H):
            step_out[g, h : h + 1, :] = dz[h * G + g : h * G + g + 1]
    rate_g = -jnp.sum(dld * dt, axis=1, keepdims=True) * rate
    bias_g = jnp.sum(dz, axis=1, keepdims=True)
    lane = lax.broadcasted_iota(jnp.int32, (gh, 128), 1)
    skip_all = jnp.concatenate([skiprow[g] for g in range(G)], axis=0)
    skip_g = jnp.concatenate(
        [
            jnp.sum(jnp.where(lane_head == h, skip_all, 0.0), axis=1, keepdims=True)
            for h in range(H)
        ],
        axis=0,
    )
    sbuf[me_p] = jnp.where(
        lane == 0, rate_g, jnp.where(lane == 1, bias_g, jnp.where(lane == 2, skip_g, 0.0))
    )

    def send_p(j):
        to = lax.rem(me_p + j, npar)
        return pltpu.make_async_remote_copy(
            src_ref=sbuf.at[me_p], dst_ref=sbuf.at[me_p],
            send_sem=p_send.at[j], recv_sem=p_recv.at[me_p],
            device_id={"seq": to // ndp, "dp": lax.rem(to, ndp)}, device_id_type=MESH,
        )

    @pl.loop(1, npar)
    def _(j):
        send_p(j).start()

    for buf, dst in ((ybuf, y_out), (dxbuf, dx_out)):
        for g in range(G):
            wide[pl.ds(g, L, stride=G), :hp] = buf[g]
        dst[...] = wide[:, :hp].astype(BF16)

    for a in range(gl):
        g = me_m * gl + a
        if pairs > 1:

            @pl.loop(1, pairs)
            def _(j):
                frm = lax.rem(me_x + j, pairs)
                pltpu.make_async_copy(part.at[g], rbuf.at[a, frm], m_recv.at[a, frm]).wait()
                part[g] = part[g] + rbuf[a, frm]

        db_out[a] = part[g, 0]
        dc_out[a] = part[g, 1]

    @pl.loop(1, npar)
    def _(j):
        frm = lax.rem(me_p + j, npar)
        pltpu.make_async_copy(sbuf.at[frm], sbuf.at[frm], p_recv.at[frm]).wait()

    total = sbuf[0]
    for j in range(1, npar):
        total = total + sbuf[j]
    turned = total.T
    for q in range(3):
        for h in range(H):
            small_out[q, h : h + 1, :] = turned[q : q + 1, h * G : (h + 1) * G]

    @pl.loop(1, npar)
    def _(j):
        send_p(j).wait_send()

    @pl.loop(0, G)
    def _(g):
        if fan > 1:

            @pl.when(jnp.logical_not(mine_c(g)))
            def _():
                send_x(g).wait_send()

        if pairs > 1:

            @pl.when(mine_c(g) & jnp.logical_not(mine_x(g)))
            def _():
                send_m(g).wait_send()

        if nseq > 1:

            @pl.when(me_s < last)
            def _():
                send_f(g).wait_send()

            @pl.when(me_s > 0)
            def _():
                send_b(g).wait_send()


def leave(y, dx, db, dc, step, small, y_out, dx_out, db_out, dc_out, step_out, *small_outs):
    y_out[...] = y[...]
    dx_out[...] = dx[...]
    for src, dst in ((db, db_out), (dc, dc_out)):
        dst[...] = jnp.stack([src[a] for a in range(src.shape[0])], axis=1).astype(BF16)
    step_out[...] = step[...]
    for q, dst in enumerate(small_outs):
        dst[...] = small[q]


def local(
    nseq, ndp, nmp,
    features, key_projection, query_proj, step_raw, doc_starts,
    log_rate, step_bias, skip_gain, out_grad,
):
    rows, L, G, hp = features.shape
    assert rows == 1
    N = key_projection.shape[-1]
    H = hp // P_SIZE
    gl = G // nmp
    gh = G * H
    npar = nseq * ndp
    raw = jnp.transpose(step_raw[0], (1, 2, 0))
    pairs = nmp // (2 if nmp % 2 == 0 else 1)
    npr = -(-3 * H // 8) * 8
    vm = pltpu.VMEM
    nr = -(-4 * H // 8) * 8
    dma = pltpu.SemaphoreType.DMA
    scratch = [
        vm((npr, 128), F32), vm((G, hp), F32),
        vm((L * G, max(hp, N)), F32),
        vm((G, L, hp), BF16), vm((G, L, N), BF16), vm((G, L, N), BF16), vm((G, L, hp), BF16),
        vm((G, N, L), BF16), vm((G, N, L), BF16), vm((G, hp, L), BF16),
        vm((G, nr, L), F32), vm((L, L), F32), vm((G, 1, hp), F32),
        vm((G, N, hp), F32), vm((G, N, hp), F32),
        vm((G, N, hp), F32), vm((G, N, hp), F32), vm((G, N, hp), F32), vm((G, N, hp), F32),
        vm((G, L, hp), F32), vm((G, L, hp), F32), vm((G, 2, L, N), F32),
        vm((G, 8, L), F32), vm((G, 8, L), F32), vm((G, 1, hp), F32), vm((G, 1, hp), F32),
        vm((G, 2, L, N), F32), vm((gl, pairs, 2, L, N), F32), vm((npar, gh, 128), F32),
        dma((G,)), dma((G,)), dma((G,)), dma((G,)), dma((G,)), dma((G,)), dma((G,)), dma((gl, pairs)),
        dma((npar,)), dma((npar,)),
    ]
    made = pl.pallas_call(
        functools.partial(kernel, nseq, ndp, nmp, L, G, H, N),
        out_shape=(
            jax.ShapeDtypeStruct((L * G, hp), BF16),
            jax.ShapeDtypeStruct((L * G, hp), BF16),
            jax.ShapeDtypeStruct((gl, L, N), F32),
            jax.ShapeDtypeStruct((gl, L, N), F32),
            jax.ShapeDtypeStruct((G, H, L), F32),
            jax.ShapeDtypeStruct((3, H, G), F32),
        ),
        in_specs=[pl.BlockSpec(memory_space=pltpu.VMEM)] * 9,
        out_specs=[pl.BlockSpec(memory_space=pltpu.VMEM)] * 6,
        scratch_shapes=scratch,
        compiler_params=pltpu.CompilerParams(
            collective_id=0, has_side_effects=True, vmem_limit_bytes=56 * 2**20
        ),
    )(
        features.reshape(L * G, hp),
        key_projection.reshape(L * G, N),
        query_proj.reshape(L * G, N),
        out_grad.reshape(L * G, hp),
        raw, doc_starts, log_rate.T, step_bias.T, skip_gain.T,
    )
    y, dx, db, dc, step, rate, bias, gain = pl.pallas_call(
        leave,
        out_shape=(
            jax.ShapeDtypeStruct((L * G, hp), BF16),
            jax.ShapeDtypeStruct((L * G, hp), BF16),
            jax.ShapeDtypeStruct((L, gl, N), BF16),
            jax.ShapeDtypeStruct((L, gl, N), BF16),
            jax.ShapeDtypeStruct((G, H, L), F32),
            jax.ShapeDtypeStruct((H, G), F32),
            jax.ShapeDtypeStruct((H, G), F32),
            jax.ShapeDtypeStruct((H, G), F32),
        ),
        in_specs=[pl.BlockSpec(memory_space=pltpu.VMEM)] * 6,
        out_specs=[pl.BlockSpec(memory_space=pltpu.VMEM)] * 8,
        compiler_params=pltpu.CompilerParams(vmem_limit_bytes=32 * 2**20),
    )(*made)
    return (
        y.reshape(1, L, G, hp),
        dx.reshape(1, L, G, hp),
        db[None],
        dc[None],
        jnp.transpose(step, (2, 0, 1))[None],
        rate.T,
        bias.T,
        gain.T,
    )


def solution(mesh):
    sizes = dict(mesh.shape)
    return jax.shard_map(
        functools.partial(local, sizes["seq"], sizes["dp"], sizes["mp"]),
        mesh=mesh,
        in_specs=(
            P("dp", "seq", None, "mp"),
            P("dp", "seq", None, None),
            P("dp", "seq", None, None),
            P("dp", "seq", None, "mp"),
            P("dp", "seq"),
            P(None, "mp"),
            P(None, "mp"),
            P(None, "mp"),
            P("dp", "seq", None, "mp"),
        ),
        out_specs=(
            P("dp", "seq", None, "mp"),
            P("dp", "seq", None, "mp"),
            P("dp", "seq", "mp", None),
            P("dp", "seq", "mp", None),
            P("dp", "seq", None, "mp"),
            P(None, "mp"),
            P(None, "mp"),
            P(None, "mp"),
        ),
        check_vma=False,
    )
```

```python
import functools

import jax
import jax.numpy as jnp
from jax import lax
from jax.experimental import pallas as pl
from jax.experimental.pallas import tpu as pltpu
from jax.sharding import PartitionSpec as P

P_SIZE = 64
F32 = jnp.float32
BF16 = jnp.bfloat16
MESH = pl.DeviceIdType.MESH
NN = ((1,), (0,))
NT = ((1,), (1,))


def mm(a, b, dims=NN):
    return lax.dot_general(a, b, (dims, ((), ())), preferred_element_type=F32)


def split2(a):
    hi = a.astype(BF16)
    return hi, (a - hi.astype(F32)).astype(BF16)


def split3(a):
    hi = a.astype(BF16)
    rest = a - hi.astype(F32)
    mid = rest.astype(BF16)
    return hi, mid, (rest - mid.astype(F32)).astype(BF16)


def left2(a, b, dims=NN):
    hi, lo = split2(a)
    return mm(hi, b, dims) + mm(lo, b, dims)


def right2(a, b, dims=NN):
    hi, lo = split2(b)
    return mm(a, hi, dims) + mm(a, lo, dims)


def left3(a, b, dims=NN):
    hi, mid, lo = split3(a)
    return mm(hi, b, dims) + mm(mid, b, dims) + mm(lo, b, dims)


def right3(a, b, dims=NN):
    hi, mid, lo = split3(b)
    return mm(a, hi, dims) + mm(a, mid, dims) + mm(a, lo, dims)


def both2(a, b, dims=NN):
    ah, al = split2(a)
    bh, bl = split2(b)
    return mm(ah, bh, dims) + mm(al, bh, dims) + mm(ah, bl, dims)


def kernel(
    nseq, ndp, nmp, L, G, H, N,
    x_ref, b_ref, c_ref, dy_ref, raw_ref, doc_ref, rate_ref, bias_ref, skip_ref,
    y_out, dx_out, db_out, dc_out, step_out, small_out,
    pars, gains,
    wide, wb, wc, wd, xg, bg, cg, gg, bt, ct, gt, tab, mask, prow,
    loc_f, loc_b, s_in, s_out, d_out, d_in,
    ybuf, dxbuf, part, rows_r, rows_k, zrow, skiprow,
    xbuf, rbuf, sbuf,
    f_send, f_recv, b_send, b_recv, x_send, x_recv, m_send, m_recv, p_send, p_recv,
):
    hp = H * P_SIZE
    gl = G // nmp
    npar = nseq * ndp
    gh = G * H
    me_s, me_d, me_m = lax.axis_index("seq"), lax.axis_index("dp"), lax.axis_index("mp")
    me_p = me_s * ndp + me_d
    last = nseq - 1
    fan = 2 if nmp % 2 == 0 else 1
    pairs = nmp // fan
    me_x, me_c = me_m // fan, lax.rem(me_m, fan)

    def at(p):
        return lax.rem(p + (me_x + 1) * (gl * fan), G)


    barrier = pltpu.get_barrier_semaphore()

    @pl.loop(1, nmp)
    def _(j):
        pl.semaphore_signal(
            barrier, inc=1, device_id={"mp": lax.rem(me_m + j, nmp)}, device_id_type=MESH
        )

    @pl.loop(1, npar)
    def _(j):
        to = lax.rem(me_p + j, npar)
        pl.semaphore_signal(
            barrier,
            inc=1,
            device_id={"seq": to // ndp, "dp": lax.rem(to, ndp)},
            device_id_type=MESH,
        )

    i0 = lax.broadcasted_iota(jnp.int32, (L, L), 0)
    i1 = lax.broadcasted_iota(jnp.int32, (L, L), 1)
    upper = jnp.where(i0 <= i1, 1.0, 0.0).astype(BF16)
    raw = jnp.concatenate([raw_ref[g, h : h + 1, :] for h in range(H) for g in range(G)], axis=0)
    pars[...] = jnp.zeros_like(pars)
    for q, ref in enumerate((rate_ref, bias_ref, skip_ref)):
        pars[q * H : (q + 1) * H, 0:G] = ref[...]
    turned = pars[...].T
    log_rate = jnp.concatenate([turned[0:G, h : h + 1] for h in range(H)], axis=0)
    bias = jnp.concatenate([turned[0:G, H + h : H + h + 1] for h in range(H)], axis=0)
    z = raw + bias
    dt = jnp.maximum(z, 0.0) + jnp.log1p(jnp.exp(-jnp.abs(z)))
    rate = jnp.exp(log_rate)
    cum = left3(-dt * rate, upper)
    docs = mm(jnp.broadcast_to(doc_ref[...].astype(F32), (8, L)).astype(BF16), upper)
    doc_row = docs[0:1]
    entry = jnp.where(doc_row == 0.0, jnp.exp(cum), 0.0)
    tail = doc_row == doc_row[:, L - 1 : L]
    weight = jnp.where(tail, jnp.exp(cum[:, L - 1 : L] - cum), 0.0) * dt
    doc_col = docs.T[:, 0:1]
    mask[...] = jnp.where((i0 >= i1) & (doc_col == doc_row), 0.0, -1e30)
    lane_head = lax.broadcasted_iota(jnp.int32, (1, hp), 1) // P_SIZE
    for g in range(G):
        for q, val in enumerate((cum, dt, weight, entry)):
            for h in range(H):
                tab[g, q * H + h : q * H + h + 1, :] = val[h * G + g : h * G + g + 1]
        passed = entry[g : g + 1, L - 1 : L]
        passed = jnp.broadcast_to(passed, (1, hp))
        for h in range(1, H):
            passed = jnp.where(
                lane_head == h, entry[h * G + g : h * G + g + 1, L - 1 : L], passed
            )
        prow[g] = passed
    gain = jnp.broadcast_to(turned[0:G, 2 * H : 2 * H + 1], (G, hp))
    for h in range(1, H):
        gain = jnp.where(lane_head == h, turned[0:G, 2 * H + h : 2 * H + h + 1], gain)
    gains[...] = gain

    lanes_l = lax.broadcasted_iota(jnp.int32, (L, hp), 1) // P_SIZE

    def spread(cols, first):
        val = jnp.broadcast_to(cols[:, first : first + 1], (L, hp))
        for h in range(1, H):
            val = jnp.where(lanes_l == h, cols[:, first + h : first + h + 1], val)
        return val

    def send_f(g):
        return pltpu.make_async_remote_copy(
            src_ref=s_out.at[g], dst_ref=s_in.at[g],
            send_sem=f_send.at[g], recv_sem=f_recv.at[g],
            device_id={"seq": jnp.minimum(me_s + 1, last)}, device_id_type=MESH,
        )

    def send_b(g):
        return pltpu.make_async_remote_copy(
            src_ref=d_in.at[g], dst_ref=d_out.at[g],
            send_sem=b_send.at[g], recv_sem=b_recv.at[g],
            device_id={"seq": jnp.maximum(me_s - 1, 0)}, device_id_type=MESH,
        )

    def send_x(g):
        return pltpu.make_async_remote_copy(
            src_ref=part.at[g], dst_ref=xbuf.at[g],
            send_sem=x_send.at[g], recv_sem=x_recv.at[g],
            device_id={"mp": me_x * fan + (fan - 1 - me_c)}, device_id_type=MESH,
        )

    def send_m(g):
        return pltpu.make_async_remote_copy(
            src_ref=part.at[g], dst_ref=rbuf.at[lax.rem(g, gl), me_x],
            send_sem=m_send.at[g], recv_sem=m_recv.at[lax.rem(g, gl), me_x],
            device_id={"mp": g // gl}, device_id_type=MESH,
        )

    def mine_c(g):
        return lax.rem(g // gl, fan) == me_c

    def mine_x(g):
        return g // (gl * fan) == me_x

    stages = ((x_ref, wide, xg, None), (b_ref, wb, bg, bt), (c_ref, wc, cg, ct), (dy_ref, wd, gg, gt))
    for src, buf, _, _ in stages:
        buf[:, : src.shape[1]] = src[...].astype(F32)
    pl.semaphore_wait(barrier, (nmp - 1) + (npar - 1))

    @pl.loop(0, G)
    def _(p):
        g = at(p)
        cols = tab[g].T
        for src, buf, dst, turned_dst in stages:
            block = buf[pl.ds(g, L, stride=G), : src.shape[1]]
            dst[g] = block.astype(BF16)
            if turned_dst is not None:
                turned_dst[g] = block.T.astype(BF16)
            if src is x_ref:
                xw = block * spread(cols, 2 * H)
            if src is dy_ref:
                gw = block * spread(cols, 3 * H)
        loc_f[g] = right2(bt[g], xw)
        loc_b[g] = right2(ct[g], gw)

        @pl.when(me_s == 0)
        def _():
            s_in[g] = jnp.zeros((N, hp), F32)
            s_out[g] = loc_f[g]
            if nseq > 1:
                send_f(g).start()

        @pl.when(me_s == last)
        def _():
            d_out[g] = jnp.zeros((N, hp), F32)
            d_in[g] = loc_b[g]
            if nseq > 1:
                send_b(g).start()

    def local(g):
        cols = tab[g].T
        trow = tab[g]
        xb, bb, cb, gb = xg[g], bg[g], cg[g], gg[g]
        scores = mm(cb, bt[g])
        grad_s = None
        y = None
        dxt = []
        pr = jnp.zeros((8, L), F32)
        head_row = lax.broadcasted_iota(jnp.int32, (8, 128), 0)
        for h in range(H):
            xm = jnp.where(lanes_l == h, xb.astype(F32), 0.0).astype(BF16)
            dm = mm(gb, xm, NT)
            decay = jnp.exp(cols[:, h : h + 1] - trow[h : h + 1] + mask[...])
            w = decay * trow[H + h : H + h + 1]
            mix = scores * w
            dmw = dm * w
            grad_s = dmw if grad_s is None else grad_s + dmw
            q = dmw * scores
            rows_k[g, h : h + 1, :] = jnp.sum(q, axis=0, keepdims=True)
            folded = q[:, 0:128]
            for j in range(128, L, 128):
                folded = folded + q[:, j : j + 128]
            pick = jnp.where(head_row == h, 1.0, 0.0).astype(BF16)
            pr = pr + right3(pick, folded, NT)
            hi, lo = split2(mix)
            now = mm(hi, xm) + mm(lo, xm)
            y = now if y is None else y + now
            gth = gt[g, h * P_SIZE : (h + 1) * P_SIZE, :]
            dxt.append(mm(gth, hi) + mm(gth, lo))
        rows_r[g] = pr
        ybuf[g] = y
        dxbuf[g] = (dxt[0] if H == 1 else jnp.concatenate(dxt, axis=0)).T
        hi, lo = split2(grad_s)
        part[g, 1] = mm(hi, bb) + mm(lo, bb)
        part[g, 0] = (mm(ct[g], hi) + mm(ct[g], lo)).T

    head8 = lax.broadcasted_iota(jnp.int32, (8, hp), 0)
    sel = jnp.where(head8 == lax.broadcasted_iota(jnp.int32, (8, hp), 1) // P_SIZE, 1.0, 0.0)
    sel = sel.astype(BF16)

    def finish(g):
        cols = tab[g].T
        wl, el = spread(cols, 2 * H), spread(cols, 3 * H)
        xb, bb, cb, gb = xg[g], bg[g], cg[g], gg[g]
        xf, gf = xb.astype(F32), gb.astype(F32)
        sin, dso = s_in[g], d_out[g]
        gain = gains[pl.ds(g, 1), :]
        yo = right2(cb, sin) * el
        dxo = right2(bb, dso) * wl
        ybuf[g] = ybuf[g] + yo + gain * xf
        dxbuf[g] = dxbuf[g] + dxo + gain * gf
        e_rows = right3(sel, gf * yo, NT)
        f_rows = right3(sel, xf * dxo, NT)
        rows_r[g] = rows_r[g] + e_rows
        rows_k[g, 0:H, :] = rows_k[g, 0:H, :] + f_rows[0:H]
        part[g, 1] = part[g, 1] + both2(gf * el, sin, NT)
        part[g, 0] = part[g, 0] + both2(xf * wl, dso, NT)
        skiprow[g] = jnp.sum(gf * xf, axis=0, keepdims=True)
        zrow[g] = jnp.sum((prow[g] * sin + loc_f[g]) * dso, axis=0, keepdims=True)

        if fan > 1:

            @pl.when(jnp.logical_not(mine_c(g)))
            def _():
                send_x(g).start()

    def across(g):
        @pl.when(mine_c(g))
        def _():
            if fan > 1:
                send_x(g).wait_recv()
                part[g] = part[g] + xbuf[g]
            if pairs > 1:

                @pl.when(jnp.logical_not(mine_x(g)))
                def _():
                    send_m(g).start()

    hop = 3
    lag_f = (me_s - 1) * hop
    lag_b = (last - me_s - 1) * hop
    lag = jnp.maximum(jnp.maximum(lag_f, lag_b), 0)

    @pl.loop(0, G + hop * max(nseq - 2, 0) + 1)
    def _(i):
        @pl.when(i < G)
        def _():
            local(at(i))

        if nseq > 1:
            pf = i - lag_f
            pb = i - lag_b

            @pl.when((me_s > 0) & (pf >= 0) & (pf < G))
            def _():
                gf = at(pf)
                send_f(gf).wait_recv()

                @pl.when(me_s < last)
                def _():
                    s_out[gf] = prow[gf] * s_in[gf] + loc_f[gf]
                    send_f(gf).start()

            @pl.when((me_s < last) & (pb >= 0) & (pb < G))
            def _():
                gb = at(pb)
                send_b(gb).wait_recv()

                @pl.when(me_s > 0)
                def _():
                    d_in[gb] = prow[gb] * d_out[gb] + loc_b[gb]
                    send_b(gb).start()

        p = i - lag

        @pl.when((p >= 0) & (p < G))
        def _():
            finish(at(p))

        @pl.when((p >= 1) & (p <= G))
        def _():
            across(at(p - 1))

    k_all = jnp.concatenate([rows_k[g, h : h + 1, :] for h in range(H) for g in range(G)], axis=0)
    r_all = jnp.concatenate([rows_r[g, h : h + 1, :] for h in range(H) for g in range(G)], axis=0)
    zcol = jnp.concatenate(
        [
            jnp.sum(jnp.where(lane_head == h, zrow[g], 0.0), axis=1, keepdims=True)
            for h in range(H)
            for g in range(G)
        ],
        axis=0,
    )
    dld = left3(r_all - k_all, upper, NT) + zcol
    ddt = k_all / dt - rate * dld
    dz = ddt * (1.0 / (1.0 + jnp.exp(-z)))
    for g in range(G):
        for h in range(H):
            step_out[g, h : h + 1, :] = dz[h * G + g : h * G + g + 1]
    rate_g = -jnp.sum(dld * dt, axis=1, keepdims=True) * rate
    bias_g = jnp.sum(dz, axis=1, keepdims=True)
    lane = lax.broadcasted_iota(jnp.int32, (gh, 128), 1)
    skip_all = jnp.concatenate([skiprow[g] for g in range(G)], axis=0)
    skip_g = jnp.concatenate(
        [
            jnp.sum(jnp.where(lane_head == h, skip_all, 0.0), axis=1, keepdims=True)
            for h in range(H)
        ],
        axis=0,
    )
    sbuf[me_p] = jnp.where(
        lane == 0, rate_g, jnp.where(lane == 1, bias_g, jnp.where(lane == 2, skip_g, 0.0))
    )

    def send_p(j):
        to = lax.rem(me_p + j, npar)
        return pltpu.make_async_remote_copy(
            src_ref=sbuf.at[me_p], dst_ref=sbuf.at[me_p],
            send_sem=p_send.at[j], recv_sem=p_recv.at[me_p],
            device_id={"seq": to // ndp, "dp": lax.rem(to, ndp)}, device_id_type=MESH,
        )

    @pl.loop(1, npar)
    def _(j):
        send_p(j).start()

    for buf, dst in ((ybuf, y_out), (dxbuf, dx_out)):
        for g in range(G):
            wide[pl.ds(g, L, stride=G), :hp] = buf[g]
        dst[...] = wide[:, :hp].astype(BF16)

    for a in range(gl):
        g = me_m * gl + a
        if pairs > 1:

            @pl.loop(1, pairs)
            def _(j):
                frm = lax.rem(me_x + j, pairs)
                pltpu.make_async_copy(part.at[g], rbuf.at[a, frm], m_recv.at[a, frm]).wait()
                part[g] = part[g] + rbuf[a, frm]

        db_out[a] = part[g, 0]
        dc_out[a] = part[g, 1]

    @pl.loop(1, npar)
    def _(j):
        frm = lax.rem(me_p + j, npar)
        pltpu.make_async_copy(sbuf.at[frm], sbuf.at[frm], p_recv.at[frm]).wait()

    total = sbuf[0]
    for j in range(1, npar):
        total = total + sbuf[j]
    turned = total.T
    for q in range(3):
        for h in range(H):
            small_out[q, h : h + 1, :] = turned[q : q + 1, h * G : (h + 1) * G]

    @pl.loop(1, npar)
    def _(j):
        send_p(j).wait_send()

    @pl.loop(0, G)
    def _(g):
        if fan > 1:

            @pl.when(jnp.logical_not(mine_c(g)))
            def _():
                send_x(g).wait_send()

        if pairs > 1:

            @pl.when(mine_c(g) & jnp.logical_not(mine_x(g)))
            def _():
                send_m(g).wait_send()

        if nseq > 1:

            @pl.when(me_s < last)
            def _():
                send_f(g).wait_send()

            @pl.when(me_s > 0)
            def _():
                send_b(g).wait_send()


def leave(y, dx, db, dc, step, small, y_out, dx_out, db_out, dc_out, step_out, *small_outs):
    y_out[...] = y[...]
    dx_out[...] = dx[...]
    for src, dst in ((db, db_out), (dc, dc_out)):
        dst[...] = jnp.stack([src[a] for a in range(src.shape[0])], axis=1).astype(BF16)
    step_out[...] = step[...]
    for q, dst in enumerate(small_outs):
        dst[...] = small[q]


def local(
    nseq, ndp, nmp,
    features, key_projection, query_proj, step_raw, doc_starts,
    log_rate, step_bias, skip_gain, out_grad,
):
    rows, L, G, hp = features.shape
    assert rows == 1
    N = key_projection.shape[-1]
    H = hp // P_SIZE
    gl = G // nmp
    gh = G * H
    npar = nseq * ndp
    raw = jnp.transpose(step_raw[0], (1, 2, 0))
    pairs = nmp // (2 if nmp % 2 == 0 else 1)
    npr = -(-3 * H // 8) * 8
    vm = pltpu.VMEM
    nr = -(-4 * H // 8) * 8
    dma = pltpu.SemaphoreType.DMA
    scratch = [
        vm((npr, 128), F32), vm((G, hp), F32),
        vm((L * G, hp), F32), vm((L * G, N), F32), vm((L * G, N), F32), vm((L * G, hp), F32),
        vm((G, L, hp), BF16), vm((G, L, N), BF16), vm((G, L, N), BF16), vm((G, L, hp), BF16),
        vm((G, N, L), BF16), vm((G, N, L), BF16), vm((G, hp, L), BF16),
        vm((G, nr, L), F32), vm((L, L), F32), vm((G, 1, hp), F32),
        vm((G, N, hp), F32), vm((G, N, hp), F32),
        vm((G, N, hp), F32), vm((G, N, hp), F32), vm((G, N, hp), F32), vm((G, N, hp), F32),
        vm((G, L, hp), F32), vm((G, L, hp), F32), vm((G, 2, L, N), F32),
        vm((G, 8, L), F32), vm((G, 8, L), F32), vm((G, 1, hp), F32), vm((G, 1, hp), F32),
        vm((G, 2, L, N), F32), vm((gl, pairs, 2, L, N), F32), vm((npar, gh, 128), F32),
        dma((G,)), dma((G,)), dma((G,)), dma((G,)), dma((G,)), dma((G,)), dma((G,)), dma((gl, pairs)),
        dma((npar,)), dma((npar,)),
    ]
    made = pl.pallas_call(
        functools.partial(kernel, nseq, ndp, nmp, L, G, H, N),
        out_shape=(
            jax.ShapeDtypeStruct((L * G, hp), BF16),
            jax.ShapeDtypeStruct((L * G, hp), BF16),
            jax.ShapeDtypeStruct((gl, L, N), F32),
            jax.ShapeDtypeStruct((gl, L, N), F32),
            jax.ShapeDtypeStruct((G, H, L), F32),
            jax.ShapeDtypeStruct((3, H, G), F32),
        ),
        in_specs=[pl.BlockSpec(memory_space=pltpu.VMEM)] * 9,
        out_specs=[pl.BlockSpec(memory_space=pltpu.VMEM)] * 6,
        scratch_shapes=scratch,
        compiler_params=pltpu.CompilerParams(
            collective_id=0, has_side_effects=True, vmem_limit_bytes=56 * 2**20
        ),
    )(
        features.reshape(L * G, hp),
        key_projection.reshape(L * G, N),
        query_proj.reshape(L * G, N),
        out_grad.reshape(L * G, hp),
        raw, doc_starts, log_rate.T, step_bias.T, skip_gain.T,
    )
    y, dx, db, dc, step, rate, bias, gain = pl.pallas_call(
        leave,
        out_shape=(
            jax.ShapeDtypeStruct((L * G, hp), BF16),
            jax.ShapeDtypeStruct((L * G, hp), BF16),
            jax.ShapeDtypeStruct((L, gl, N), BF16),
            jax.ShapeDtypeStruct((L, gl, N), BF16),
            jax.ShapeDtypeStruct((G, H, L), F32),
            jax.ShapeDtypeStruct((H, G), F32),
            jax.ShapeDtypeStruct((H, G), F32),
            jax.ShapeDtypeStruct((H, G), F32),
        ),
        in_specs=[pl.BlockSpec(memory_space=pltpu.VMEM)] * 6,
        out_specs=[pl.BlockSpec(memory_space=pltpu.VMEM)] * 8,
        compiler_params=pltpu.CompilerParams(vmem_limit_bytes=60 * 2**20),
    )(*made)
    return (
        y.reshape(1, L, G, hp),
        dx.reshape(1, L, G, hp),
        db[None],
        dc[None],
        jnp.transpose(step, (2, 0, 1))[None],
        rate.T,
        bias.T,
        gain.T,
    )


def solution(mesh):
    sizes = dict(mesh.shape)
    return jax.shard_map(
        functools.partial(local, sizes["seq"], sizes["dp"], sizes["mp"]),
        mesh=mesh,
        in_specs=(
            P("dp", "seq", None, "mp"),
            P("dp", "seq", None, None),
            P("dp", "seq", None, None),
            P("dp", "seq", None, "mp"),
            P("dp", "seq"),
            P(None, "mp"),
            P(None, "mp"),
            P(None, "mp"),
            P("dp", "seq", None, "mp"),
        ),
        out_specs=(
            P("dp", "seq", None, "mp"),
            P("dp", "seq", None, "mp"),
            P("dp", "seq", "mp", None),
            P("dp", "seq", "mp", None),
            P("dp", "seq", None, "mp"),
            P(None, "mp"),
            P(None, "mp"),
            P(None, "mp"),
        ),
        check_vma=False,
    )
```

```python
import functools

import jax
import jax.numpy as jnp
from jax import lax
from jax.experimental import pallas as pl
from jax.experimental.pallas import tpu as pltpu
from jax.sharding import PartitionSpec as P

P_SIZE = 64
F32 = jnp.float32
BF16 = jnp.bfloat16
MESH = pl.DeviceIdType.MESH
NN = ((1,), (0,))
NT = ((1,), (1,))


def mm(a, b, dims=NN):
    return lax.dot_general(a, b, (dims, ((), ())), preferred_element_type=F32)


def split2(a):
    hi = a.astype(BF16)
    return hi, (a - hi.astype(F32)).astype(BF16)


def split3(a):
    hi = a.astype(BF16)
    rest = a - hi.astype(F32)
    mid = rest.astype(BF16)
    return hi, mid, (rest - mid.astype(F32)).astype(BF16)


def left2(a, b, dims=NN):
    hi, lo = split2(a)
    return mm(hi, b, dims) + mm(lo, b, dims)


def right2(a, b, dims=NN):
    hi, lo = split2(b)
    return mm(a, hi, dims) + mm(a, lo, dims)


def left3(a, b, dims=NN):
    hi, mid, lo = split3(a)
    return mm(hi, b, dims) + mm(mid, b, dims) + mm(lo, b, dims)


def right3(a, b, dims=NN):
    hi, mid, lo = split3(b)
    return mm(a, hi, dims) + mm(a, mid, dims) + mm(a, lo, dims)


def both2(a, b, dims=NN):
    ah, al = split2(a)
    bh, bl = split2(b)
    return mm(ah, bh, dims) + mm(al, bh, dims) + mm(ah, bl, dims)


def kernel(
    nseq, ndp, nmp, L, G, H, N,
    x_ref, b_ref, c_ref, dy_ref, raw_ref, doc_ref, rate_ref, bias_ref, skip_ref,
    y_out, dx_out, db_out, dc_out, step_out, small_out,
    pars, gains,
    wide, wb, wc, wd, xg, bg, cg, gg, bt, ct, gt, tab, mask, prow,
    loc_f, loc_b, s_in, s_out, d_out, d_in,
    ybuf, dxbuf, part, rows_r, rows_k, zrow, skiprow,
    xbuf, rbuf, sbuf,
    f_send, f_recv, b_send, b_recv, x_send, x_recv, m_send, m_recv, p_send, p_recv,
):
    hp = H * P_SIZE
    gl = G // nmp
    npar = nseq * ndp
    gh = G * H
    me_s, me_d, me_m = lax.axis_index("seq"), lax.axis_index("dp"), lax.axis_index("mp")
    me_p = me_s * ndp + me_d
    last = nseq - 1
    fan = 2 if nmp % 2 == 0 else 1
    pairs = nmp // fan
    me_x, me_c = me_m // fan, lax.rem(me_m, fan)

    def at(p):
        return lax.rem(p + (me_x + 1) * (gl * fan), G)


    barrier = pltpu.get_barrier_semaphore()

    @pl.loop(1, nmp)
    def _(j):
        pl.semaphore_signal(
            barrier, inc=1, device_id={"mp": lax.rem(me_m + j, nmp)}, device_id_type=MESH
        )

    @pl.loop(1, npar)
    def _(j):
        to = lax.rem(me_p + j, npar)
        pl.semaphore_signal(
            barrier,
            inc=1,
            device_id={"seq": to // ndp, "dp": lax.rem(to, ndp)},
            device_id_type=MESH,
        )

    i0 = lax.broadcasted_iota(jnp.int32, (L, L), 0)
    i1 = lax.broadcasted_iota(jnp.int32, (L, L), 1)
    upper = jnp.where(i0 <= i1, 1.0, 0.0).astype(BF16)
    raw = jnp.concatenate([raw_ref[g, h : h + 1, :] for h in range(H) for g in range(G)], axis=0)
    pars[...] = jnp.zeros_like(pars)
    for q, ref in enumerate((rate_ref, bias_ref, skip_ref)):
        pars[q * H : (q + 1) * H, 0:G] = ref[...]
    turned = pars[...].T
    log_rate = jnp.concatenate([turned[0:G, h : h + 1] for h in range(H)], axis=0)
    bias = jnp.concatenate([turned[0:G, H + h : H + h + 1] for h in range(H)], axis=0)
    z = raw + bias
    dt = jnp.maximum(z, 0.0) + jnp.log1p(jnp.exp(-jnp.abs(z)))
    rate = jnp.exp(log_rate)
    cum = left3(-dt * rate, upper)
    docs = mm(jnp.broadcast_to(doc_ref[...].astype(F32), (8, L)).astype(BF16), upper)
    doc_row = docs[0:1]
    entry = jnp.where(doc_row == 0.0, jnp.exp(cum), 0.0)
    tail = doc_row == doc_row[:, L - 1 : L]
    weight = jnp.where(tail, jnp.exp(cum[:, L - 1 : L] - cum), 0.0) * dt
    doc_col = docs.T[:, 0:1]
    mask[...] = jnp.where((i0 >= i1) & (doc_col == doc_row), 0.0, -1e30)
    lane_head = lax.broadcasted_iota(jnp.int32, (1, hp), 1) // P_SIZE
    for g in range(G):
        for q, val in enumerate((cum, dt, weight, entry)):
            for h in range(H):
                tab[g, q * H + h : q * H + h + 1, :] = val[h * G + g : h * G + g + 1]
        passed = entry[g : g + 1, L - 1 : L]
        passed = jnp.broadcast_to(passed, (1, hp))
        for h in range(1, H):
            passed = jnp.where(
                lane_head == h, entry[h * G + g : h * G + g + 1, L - 1 : L], passed
            )
        prow[g] = passed
    gain = jnp.broadcast_to(turned[0:G, 2 * H : 2 * H + 1], (G, hp))
    for h in range(1, H):
        gain = jnp.where(lane_head == h, turned[0:G, 2 * H + h : 2 * H + h + 1], gain)
    gains[...] = gain

    lanes_l = lax.broadcasted_iota(jnp.int32, (L, hp), 1) // P_SIZE

    def spread(cols, first):
        val = jnp.broadcast_to(cols[:, first : first + 1], (L, hp))
        for h in range(1, H):
            val = jnp.where(lanes_l == h, cols[:, first + h : first + h + 1], val)
        return val

    def send_f(g):
        return pltpu.make_async_remote_copy(
            src_ref=s_out.at[g], dst_ref=s_in.at[g],
            send_sem=f_send.at[g], recv_sem=f_recv.at[g],
            device_id={"seq": jnp.minimum(me_s + 1, last)}, device_id_type=MESH,
        )

    def send_b(g):
        return pltpu.make_async_remote_copy(
            src_ref=d_in.at[g], dst_ref=d_out.at[g],
            send_sem=b_send.at[g], recv_sem=b_recv.at[g],
            device_id={"seq": jnp.maximum(me_s - 1, 0)}, device_id_type=MESH,
        )

    def send_x(g):
        return pltpu.make_async_remote_copy(
            src_ref=part.at[g], dst_ref=xbuf.at[g],
            send_sem=x_send.at[g], recv_sem=x_recv.at[g],
            device_id={"mp": me_x * fan + (fan - 1 - me_c)}, device_id_type=MESH,
        )

    def send_m(g):
        return pltpu.make_async_remote_copy(
            src_ref=part.at[g], dst_ref=rbuf.at[lax.rem(g, gl), me_x],
            send_sem=m_send.at[g], recv_sem=m_recv.at[lax.rem(g, gl), me_x],
            device_id={"mp": g // gl}, device_id_type=MESH,
        )

    def mine_c(g):
        return lax.rem(g // gl, fan) == me_c

    def mine_x(g):
        return g // (gl * fan) == me_x

    stages = ((x_ref, wide, xg, None), (b_ref, wb, bg, bt), (c_ref, wc, cg, ct), (dy_ref, wd, gg, gt))
    for src, buf, _, _ in stages:
        buf[:, : src.shape[1]] = src[...].astype(F32)
    pl.semaphore_wait(barrier, (nmp - 1) + (npar - 1))

    @pl.loop(0, G)
    def _(p):
        g = at(p)
        cols = tab[g].T
        for src, buf, dst, turned_dst in stages:
            block = buf[pl.ds(g, L, stride=G), : src.shape[1]]
            dst[g] = block.astype(BF16)
            if turned_dst is not None:
                turned_dst[g] = block.T.astype(BF16)
            if src is x_ref:
                xw = block * spread(cols, 2 * H)
            if src is dy_ref:
                gw = block * spread(cols, 3 * H)
        loc_f[g] = right2(bt[g], xw)
        loc_b[g] = right2(ct[g], gw)

        @pl.when(me_s == 0)
        def _():
            s_in[g] = jnp.zeros((N, hp), F32)
            s_out[g] = loc_f[g]
            if nseq > 1:
                send_f(g).start()

        @pl.when(me_s == last)
        def _():
            d_out[g] = jnp.zeros((N, hp), F32)
            d_in[g] = loc_b[g]
            if nseq > 1:
                send_b(g).start()

    def local(g):
        cols = tab[g].T
        trow = tab[g]
        xb, bb, cb, gb = xg[g], bg[g], cg[g], gg[g]
        scores = mm(cb, bt[g])
        grad_s = None
        y = None
        dxt = []
        folds = []
        pick = lax.broadcasted_iota(jnp.int32, (8, 128 * H), 0) == (
            lax.broadcasted_iota(jnp.int32, (8, 128 * H), 1) // 128
        )
        pick = jnp.where(pick, 1.0, 0.0).astype(BF16)
        for h in range(H):
            xm = jnp.where(lanes_l == h, xb.astype(F32), 0.0).astype(BF16)
            dm = mm(gb, xm, NT)
            decay = jnp.exp(cols[:, h : h + 1] - trow[h : h + 1] + mask[...])
            w = decay * trow[H + h : H + h + 1]
            mix = scores * w
            dmw = dm * w
            grad_s = dmw if grad_s is None else grad_s + dmw
            q = dmw * scores
            rows_k[g, h : h + 1, :] = jnp.sum(q, axis=0, keepdims=True)
            folded = q[:, 0:128]
            for j in range(128, L, 128):
                folded = folded + q[:, j : j + 128]
            folds.append(folded)
            hi, lo = split2(mix)
            now = mm(hi, xm) + mm(lo, xm)
            y = now if y is None else y + now
            gth = gt[g, h * P_SIZE : (h + 1) * P_SIZE, :]
            dxt.append(mm(gth, hi) + mm(gth, lo))
        rows_r[g] = right3(pick, folds[0] if H == 1 else jnp.concatenate(folds, axis=1), NT)
        ybuf[g] = y
        dxbuf[g] = (dxt[0] if H == 1 else jnp.concatenate(dxt, axis=0)).T
        hi, lo = split2(grad_s)
        part[g, 1] = mm(hi, bb) + mm(lo, bb)
        part[g, 0] = (mm(ct[g], hi) + mm(ct[g], lo)).T

    head8 = lax.broadcasted_iota(jnp.int32, (8, 2 * hp), 0)
    sel = jnp.where(head8 == lax.broadcasted_iota(jnp.int32, (8, 2 * hp), 1) // P_SIZE, 1.0, 0.0)
    sel = sel.astype(BF16)

    def finish(g):
        cols = tab[g].T
        wl, el = spread(cols, 2 * H), spread(cols, 3 * H)
        xb, bb, cb, gb = xg[g], bg[g], cg[g], gg[g]
        xf, gf = xb.astype(F32), gb.astype(F32)
        sin, dso = s_in[g], d_out[g]
        gain = gains[pl.ds(g, 1), :]
        yo = right2(cb, sin) * el
        dxo = right2(bb, dso) * wl
        ybuf[g] = ybuf[g] + yo + gain * xf
        dxbuf[g] = dxbuf[g] + dxo + gain * gf
        ef = right3(sel, jnp.concatenate([gf * yo, xf * dxo], axis=1), NT)
        rows_r[g, 0:H, :] = rows_r[g, 0:H, :] + ef[0:H]
        rows_k[g, 0:H, :] = rows_k[g, 0:H, :] + ef[H : 2 * H]
        part[g, 1] = part[g, 1] + both2(gf * el, sin, NT)
        part[g, 0] = part[g, 0] + both2(xf * wl, dso, NT)
        skiprow[g] = jnp.sum(gf * xf, axis=0, keepdims=True)
        zrow[g] = jnp.sum((prow[g] * sin + loc_f[g]) * dso, axis=0, keepdims=True)

        if fan > 1:

            @pl.when(jnp.logical_not(mine_c(g)))
            def _():
                send_x(g).start()

    def across(g):
        @pl.when(mine_c(g))
        def _():
            if fan > 1:
                send_x(g).wait_recv()
                part[g] = part[g] + xbuf[g]
            if pairs > 1:

                @pl.when(jnp.logical_not(mine_x(g)))
                def _():
                    send_m(g).start()

    hop = 3
    lag_f = (me_s - 1) * hop
    lag_b = (last - me_s - 1) * hop
    lag = jnp.maximum(jnp.maximum(lag_f, lag_b), 0)

    @pl.loop(0, G + hop * max(nseq - 2, 0) + 1)
    def _(i):
        @pl.when(i < G)
        def _():
            local(at(i))

        if nseq > 1:
            pf = i - lag_f
            pb = i - lag_b

            @pl.when((me_s > 0) & (pf >= 0) & (pf < G))
            def _():
                gf = at(pf)
                send_f(gf).wait_recv()

                @pl.when(me_s < last)
                def _():
                    s_out[gf] = prow[gf] * s_in[gf] + loc_f[gf]
                    send_f(gf).start()

            @pl.when((me_s < last) & (pb >= 0) & (pb < G))
            def _():
                gb = at(pb)
                send_b(gb).wait_recv()

                @pl.when(me_s > 0)
                def _():
                    d_in[gb] = prow[gb] * d_out[gb] + loc_b[gb]
                    send_b(gb).start()

        p = i - lag

        @pl.when((p >= 0) & (p < G))
        def _():
            finish(at(p))

        @pl.when((p >= 1) & (p <= G))
        def _():
            across(at(p - 1))

    k_all = jnp.concatenate([rows_k[g, h : h + 1, :] for h in range(H) for g in range(G)], axis=0)
    r_all = jnp.concatenate([rows_r[g, h : h + 1, :] for h in range(H) for g in range(G)], axis=0)
    zcol = jnp.concatenate(
        [
            jnp.sum(jnp.where(lane_head == h, zrow[g], 0.0), axis=1, keepdims=True)
            for h in range(H)
            for g in range(G)
        ],
        axis=0,
    )
    dld = left3(r_all - k_all, upper, NT) + zcol
    ddt = k_all / dt - rate * dld
    dz = ddt * (1.0 / (1.0 + jnp.exp(-z)))
    for g in range(G):
        for h in range(H):
            step_out[g, h : h + 1, :] = dz[h * G + g : h * G + g + 1]
    rate_g = -jnp.sum(dld * dt, axis=1, keepdims=True) * rate
    bias_g = jnp.sum(dz, axis=1, keepdims=True)
    lane = lax.broadcasted_iota(jnp.int32, (gh, 128), 1)
    skip_all = jnp.concatenate([skiprow[g] for g in range(G)], axis=0)
    skip_g = jnp.concatenate(
        [
            jnp.sum(jnp.where(lane_head == h, skip_all, 0.0), axis=1, keepdims=True)
            for h in range(H)
        ],
        axis=0,
    )
    sbuf[me_p] = jnp.where(
        lane == 0, rate_g, jnp.where(lane == 1, bias_g, jnp.where(lane == 2, skip_g, 0.0))
    )

    def send_p(j):
        to = lax.rem(me_p + j, npar)
        return pltpu.make_async_remote_copy(
            src_ref=sbuf.at[me_p], dst_ref=sbuf.at[me_p],
            send_sem=p_send.at[j], recv_sem=p_recv.at[me_p],
            device_id={"seq": to // ndp, "dp": lax.rem(to, ndp)}, device_id_type=MESH,
        )

    @pl.loop(1, npar)
    def _(j):
        send_p(j).start()

    for buf, dst in ((ybuf, y_out), (dxbuf, dx_out)):
        for g in range(G):
            wide[pl.ds(g, L, stride=G), :hp] = buf[g]
        dst[...] = wide[:, :hp].astype(BF16)

    for a in range(gl):
        g = me_m * gl + a
        if pairs > 1:

            @pl.loop(1, pairs)
            def _(j):
                frm = lax.rem(me_x + j, pairs)
                pltpu.make_async_copy(part.at[g], rbuf.at[a, frm], m_recv.at[a, frm]).wait()
                part[g] = part[g] + rbuf[a, frm]

        db_out[a] = part[g, 0]
        dc_out[a] = part[g, 1]

    @pl.loop(1, npar)
    def _(j):
        frm = lax.rem(me_p + j, npar)
        pltpu.make_async_copy(sbuf.at[frm], sbuf.at[frm], p_recv.at[frm]).wait()

    total = sbuf[0]
    for j in range(1, npar):
        total = total + sbuf[j]
    turned = total.T
    for q in range(3):
        for h in range(H):
            small_out[q, h : h + 1, :] = turned[q : q + 1, h * G : (h + 1) * G]

    @pl.loop(1, npar)
    def _(j):
        send_p(j).wait_send()

    @pl.loop(0, G)
    def _(g):
        if fan > 1:

            @pl.when(jnp.logical_not(mine_c(g)))
            def _():
                send_x(g).wait_send()

        if pairs > 1:

            @pl.when(mine_c(g) & jnp.logical_not(mine_x(g)))
            def _():
                send_m(g).wait_send()

        if nseq > 1:

            @pl.when(me_s < last)
            def _():
                send_f(g).wait_send()

            @pl.when(me_s > 0)
            def _():
                send_b(g).wait_send()


def leave(y, dx, db, dc, step, small, y_out, dx_out, db_out, dc_out, step_out, *small_outs):
    y_out[...] = y[...]
    dx_out[...] = dx[...]
    for src, dst in ((db, db_out), (dc, dc_out)):
        dst[...] = jnp.stack([src[a] for a in range(src.shape[0])], axis=1).astype(BF16)
    step_out[...] = step[...]
    for q, dst in enumerate(small_outs):
        dst[...] = small[q]


def local(
    nseq, ndp, nmp,
    features, key_projection, query_proj, step_raw, doc_starts,
    log_rate, step_bias, skip_gain, out_grad,
):
    rows, L, G, hp = features.shape
    assert rows == 1
    N = key_projection.shape[-1]
    H = hp // P_SIZE
    gl = G // nmp
    gh = G * H
    npar = nseq * ndp
    raw = jnp.transpose(step_raw[0], (1, 2, 0))
    pairs = nmp // (2 if nmp % 2 == 0 else 1)
    npr = -(-3 * H // 8) * 8
    vm = pltpu.VMEM
    nr = -(-4 * H // 8) * 8
    dma = pltpu.SemaphoreType.DMA
    scratch = [
        vm((npr, 128), F32), vm((G, hp), F32),
        vm((L * G, hp), F32), vm((L * G, N), F32), vm((L * G, N), F32), vm((L * G, hp), F32),
        vm((G, L, hp), BF16), vm((G, L, N), BF16), vm((G, L, N), BF16), vm((G, L, hp), BF16),
        vm((G, N, L), BF16), vm((G, N, L), BF16), vm((G, hp, L), BF16),
        vm((G, nr, L), F32), vm((L, L), F32), vm((G, 1, hp), F32),
        vm((G, N, hp), F32), vm((G, N, hp), F32),
        vm((G, N, hp), F32), vm((G, N, hp), F32), vm((G, N, hp), F32), vm((G, N, hp), F32),
        vm((G, L, hp), F32), vm((G, L, hp), F32), vm((G, 2, L, N), F32),
        vm((G, 8, L), F32), vm((G, 8, L), F32), vm((G, 1, hp), F32), vm((G, 1, hp), F32),
        vm((G, 2, L, N), F32), vm((gl, pairs, 2, L, N), F32), vm((npar, gh, 128), F32),
        dma((G,)), dma((G,)), dma((G,)), dma((G,)), dma((G,)), dma((G,)), dma((G,)), dma((gl, pairs)),
        dma((npar,)), dma((npar,)),
    ]
    made = pl.pallas_call(
        functools.partial(kernel, nseq, ndp, nmp, L, G, H, N),
        out_shape=(
            jax.ShapeDtypeStruct((L * G, hp), BF16),
            jax.ShapeDtypeStruct((L * G, hp), BF16),
            jax.ShapeDtypeStruct((gl, L, N), F32),
            jax.ShapeDtypeStruct((gl, L, N), F32),
            jax.ShapeDtypeStruct((G, H, L), F32),
            jax.ShapeDtypeStruct((3, H, G), F32),
        ),
        in_specs=[pl.BlockSpec(memory_space=pltpu.VMEM)] * 9,
        out_specs=[pl.BlockSpec(memory_space=pltpu.VMEM)] * 6,
        scratch_shapes=scratch,
        compiler_params=pltpu.CompilerParams(
            collective_id=0, has_side_effects=True, vmem_limit_bytes=56 * 2**20
        ),
    )(
        features.reshape(L * G, hp),
        key_projection.reshape(L * G, N),
        query_proj.reshape(L * G, N),
        out_grad.reshape(L * G, hp),
        raw, doc_starts, log_rate.T, step_bias.T, skip_gain.T,
    )
    y, dx, db, dc, step, rate, bias, gain = pl.pallas_call(
        leave,
        out_shape=(
            jax.ShapeDtypeStruct((L * G, hp), BF16),
            jax.ShapeDtypeStruct((L * G, hp), BF16),
            jax.ShapeDtypeStruct((L, gl, N), BF16),
            jax.ShapeDtypeStruct((L, gl, N), BF16),
            jax.ShapeDtypeStruct((G, H, L), F32),
            jax.ShapeDtypeStruct((H, G), F32),
            jax.ShapeDtypeStruct((H, G), F32),
            jax.ShapeDtypeStruct((H, G), F32),
        ),
        in_specs=[pl.BlockSpec(memory_space=pltpu.VMEM)] * 6,
        out_specs=[pl.BlockSpec(memory_space=pltpu.VMEM)] * 8,
        compiler_params=pltpu.CompilerParams(vmem_limit_bytes=60 * 2**20),
    )(*made)
    return (
        y.reshape(1, L, G, hp),
        dx.reshape(1, L, G, hp),
        db[None],
        dc[None],
        jnp.transpose(step, (2, 0, 1))[None],
        rate.T,
        bias.T,
        gain.T,
    )


def solution(mesh):
    sizes = dict(mesh.shape)
    return jax.shard_map(
        functools.partial(local, sizes["seq"], sizes["dp"], sizes["mp"]),
        mesh=mesh,
        in_specs=(
            P("dp", "seq", None, "mp"),
            P("dp", "seq", None, None),
            P("dp", "seq", None, None),
            P("dp", "seq", None, "mp"),
            P("dp", "seq"),
            P(None, "mp"),
            P(None, "mp"),
            P(None, "mp"),
            P("dp", "seq", None, "mp"),
        ),
        out_specs=(
            P("dp", "seq", None, "mp"),
            P("dp", "seq", None, "mp"),
            P("dp", "seq", "mp", None),
            P("dp", "seq", "mp", None),
            P("dp", "seq", None, "mp"),
            P(None, "mp"),
            P(None, "mp"),
            P(None, "mp"),
        ),
        check_vma=False,
    )
```
